32 devices in a mesh: row: 4 (over y, x), col: 8 (over z, core).
Axes of the slice: x: 2, y: 2, z: 4, core: 2. Of those that a mesh axis runs over, the one named last changes fastest.
Arguments:
- record: bfloat16 [45056, 4096], P(('row', 'col')), may hold values from -6 to 6
- fir_taps: float32 [101], replicated, may hold values from -0.625 to 0.625
- bins: int32 [16], replicated, may hold values from 1 to 639
- offsets: int32 [32], P(('row', 'col')), may hold values from 0 to 28, as said below
Outputs:
- cross: bfloat16 [16, 2, 4096, 4096], P(None, None, 'row', 'col')
The draws below stay inside these ranges and needn't reach their ends.
Inputs may be any that keep to these rules, and one draw needn't show every extreme that they name: `offsets`: a window's start offset within its slot of 1408 samples.
All inputs are finite; a program needn't handle non-finite values.
Results may differ from the reference program's by a relative error of at most 0.0069.
Values may be sent and summed in bfloat16 or wider, within the bound.
No kernel may reach another device: no remote copies, remote signals or barrier semaphores. Data moves between devices by JAX's collectives and lax.ppermute only.
A program may use at most 192 MiB of HBM per device.

```python
import math
import jax
import jax.numpy as jnp
from jax import lax

CH = 4096
F = 16
WL = 1280
TAPS = 101
SLACK = 28
WIN_DEV = 1
SEG_DEV = 1408
NW = 32
SAMPLES = 45056


def draw_offsets(key, part):
    values = jax.random.randint(key, (NW,), 0, SLACK + 1)
    values = values.at[0].set(SLACK)
    values = values.at[NW - 1].set(0)
    return values.astype(jnp.int32)


def set_ends(drawn, rng, smallest, high):
    shape = drawn.shape
    spot = [jax.random.randint(jax.random.fold_in(rng, axis), (), 0, shape[axis]) for axis in range(len(shape))]
    drawn = drawn.at[tuple(spot)].set(smallest)
    longest = shape.index(max(shape))
    spot[longest] = (spot[longest] + 1) % shape[longest]
    return drawn.at[tuple(spot)].set(high)


def levels(stream_key, shape, split, low, high):
    loudness, own = 1.0, jax.random.fold_in(stream_key, 6)
    for dim, parts in split:
        steps = jnp.exp(jax.random.uniform(jax.random.fold_in(own, dim), (parts,), jnp.float32, low / len(split), high / len(split)))
        loudness = loudness * jnp.repeat(steps, shape[dim] // parts).reshape([-1 if axis == dim else 1 for axis in range(len(shape))])
    return loudness


def gaussian(own_key, extent, width, reach, pieces=(), kind=jnp.bfloat16):
    values = width * jax.random.normal(own_key, extent, jnp.float32)
    if pieces:
        values = values * levels(own_key, extent, pieces, -0.22, 0.18)
    return jnp.clip(values, -reach, reach).astype(kind)


def setup_inputs(seed: int = 0) -> dict:
    arg_keys = jax.random.split(jax.random.key(seed), 5)
    record = gaussian(arg_keys[0], (SAMPLES, CH), 1.0, 6.0, ((0, 32),))
    fir_taps = gaussian(arg_keys[1], (TAPS,), TAPS ** -0.5, 0.625, (), jnp.float32)
    bins = set_ends(jax.random.randint(arg_keys[2], (F,), 1, WL // 2), jax.random.fold_in(arg_keys[2], 1), 1, (WL // 2) - 1).astype(jnp.int32)
    offsets = draw_offsets(jax.random.fold_in(arg_keys[4], 71), 0)
    return {"record": record, "fir_taps": fir_taps, "bins": bins, "offsets": offsets}


floor_level = 0.5

def analysis_kernel(fir_taps, bins):
    span = WL + TAPS - 1
    sample_times = jnp.arange(WL, dtype=jnp.int32)
    phase_index = bins[:, None] * sample_times[None, :] % WL
    angles = 2.0 * math.pi / WL * phase_index.astype(jnp.float32)
    centre = (jnp.arange(WL, dtype=jnp.float32) + 0.5) / WL
    window_taper = (0.5 - 0.5 * jnp.cos(2.0 * math.pi * centre)) / math.sqrt(WL)
    pattern = jnp.stack([jnp.cos(angles) * window_taper, -jnp.sin(angles) * window_taper]).reshape(2 * F, WL)
    length = WL + span - 1
    middle = jnp.zeros((length - TAPS,), jnp.float32)
    vector = jnp.concatenate([fir_taps[TAPS - 1:], middle, fir_taps[:TAPS - 1]])
    band = jnp.tile(vector, span)[:span * (length - 1)].reshape(span, length - 1)[:, :WL]
    kernel = jnp.dot(pattern, band.T, precision=lax.Precision.HIGHEST, preferred_element_type=jnp.float32)
    return kernel.astype(jnp.bfloat16)

def whiten(spectra):
    shaped = spectra.reshape(spectra.shape[0], 2, F, spectra.shape[-1])
    magnitude = jnp.sqrt(shaped[:, 0] * shaped[:, 0] + shaped[:, 1] * shaped[:, 1])
    inverse = 1.0 / jnp.maximum(magnitude, floor_level)
    return (shaped * inverse[:, None]).astype(jnp.bfloat16)

def reference(record, fir_taps, bins, offsets):
    kernel = analysis_kernel(fir_taps, bins)
    span = WL + TAPS - 1

    def one_window(window):
        first_row = window // WIN_DEV * SEG_DEV + window % WIN_DEV * WL + offsets[window]
        samples = lax.dynamic_slice_in_dim(record, first_row.astype(jnp.int32), span, 0)
        return jnp.dot(kernel, samples, preferred_element_type=jnp.float32)
    spectra = lax.map(one_window, jnp.arange(NW, dtype=jnp.int32))
    whitened = whiten(spectra)

    def one_bin(bin_index):
        real_part = whitened[:, 0, bin_index, :]
        imag_part = whitened[:, 1, bin_index, :]
        real_sum = jnp.dot(real_part.T, real_part, preferred_element_type=jnp.float32) + jnp.dot(imag_part.T, imag_part, preferred_element_type=jnp.float32)
        imag_sum = jnp.dot(real_part.T, imag_part, preferred_element_type=jnp.float32) - jnp.dot(imag_part.T, real_part, preferred_element_type=jnp.float32)
        return (jnp.stack([real_sum, imag_sum]) / NW).astype(jnp.bfloat16)
    return lax.map(one_bin, jnp.arange(F, dtype=jnp.int32))
```

```python
import functools
import math

import jax
import jax.numpy as jnp
from jax import lax
from jax.experimental import pallas as pl
from jax.experimental.pallas import tpu as pltpu
from jax.sharding import PartitionSpec as P

F = 16
WL = 1280
TAPS = 101
SPAN = WL + TAPS - 1
LANES = 128
FLOOR = 0.5
CHUNK = 4
CHUNKS = F // CHUNK
GROUP = 2 * CHUNK
ROWS = 2 * F
CALLS = 2

AXES = ("row", "col")
BF16 = jnp.bfloat16
F32 = jnp.float32


def sine(x):
    square = x * x
    total = jnp.full_like(x, 1.0 / math.factorial(13))
    for order in (11, 9, 7, 5, 3, 1):
        sign = -1.0 if order % 4 == 3 else 1.0
        total = total * square + sign / math.factorial(order)
    return x * total


def analysis_rows(bins, pattern, stacked, taps, offset, kernel):
    depth = kernel.shape[1]
    blocks = depth // LANES
    times = lax.broadcasted_iota(jnp.int32, (1, WL), 1).astype(F32)
    row = lax.broadcasted_iota(jnp.int32, (ROWS, 1), 0)
    chosen = jnp.zeros((ROWS, 1), F32)
    for index in range(F):
        this = (row // GROUP == index // CHUNK) & (row % CHUNK == index % CHUNK)
        chosen = jnp.where(this, bins[index].astype(F32), chosen)
    quarter = jnp.where(row % GROUP < CHUNK, 0.0, WL / 4.0)
    phase = chosen * times + quarter
    phase = phase - WL * jnp.floor((phase + 0.5) * (1.0 / WL))
    half = sine((phase - WL / 2.0) * (math.pi / WL))
    edge = times + 0.5
    taper = sine(jnp.minimum(edge, WL - edge) * (math.pi / WL))
    taper = taper * taper * (1.0 / math.sqrt(WL))
    pattern[:, :LANES] = jnp.zeros((ROWS, LANES), F32)
    pattern[:, LANES + WL :] = jnp.zeros((ROWS, depth - WL), F32)
    pattern[:, LANES : LANES + WL] = (2.0 * half * half - 1.0) * taper

    slack = depth - SPAN
    lane = lax.broadcasted_iota(jnp.int32, (8, 2 * LANES), 1) - (slack - offset)
    filter_row = jnp.zeros((8, 2 * LANES), F32)
    for index in range(TAPS):
        filter_row = jnp.where(lane == index, taps[index], filter_row)
    filter_rows = jnp.concatenate([filter_row] * (LANES // 8), axis=0)
    band = pltpu.roll(filter_rows, 0, 1, stride=1, stride_axis=0)

    for block in range(blocks):
        stacked[block * ROWS : (block + 1) * ROWS, :] = pattern[
            :, block * LANES : (block + 2) * LANES
        ]
    filtered = lax.dot_general(
        stacked[...],
        band,
        (((1,), (1,)), ((), ())),
        precision=lax.Precision.HIGHEST,
        preferred_element_type=F32,
    )
    for block in range(blocks):
        kernel[:, block * LANES : (block + 1) * LANES] = filtered[
            block * ROWS : (block + 1) * ROWS
        ].astype(BF16)


def spectra_body(row_count, col_count, place, offsets, bins, taps, record, *refs):
    to_rows = refs[:row_count]
    to_cols = refs[row_count : row_count + col_count]
    samples, pattern, stacked, kernel, whitened, arrived = refs[row_count + col_count :]
    width = samples.shape[2]
    copies = []
    for block in range(col_count):
        copy = pltpu.make_async_copy(
            record.at[:, pl.ds(block * width, width)], samples.at[block], arrived.at[block]
        )
        copy.start()
        copies.append(copy)
    analysis_rows(bins, pattern, stacked, taps, offsets[0], kernel)
    for block in range(col_count):
        copies[block].wait()
        spectra = jnp.dot(kernel[...], samples[block], preferred_element_type=F32)
        shaped = spectra.reshape(CHUNKS, 2, CHUNK, width)
        real, imag = shaped[:, 0], shaped[:, 1]
        magnitude = jnp.sqrt(real * real + imag * imag)
        inverse = 1.0 / jnp.maximum(magnitude, FLOOR)
        scaled = (shaped * inverse[:, None]).reshape(ROWS, width)
        whitened[block] = scaled.astype(BF16)
    row, col = place[0], place[1]
    share = col_count // row_count
    for step in range(row_count):
        for part in range(share):
            to_rows[step][:, part * width : (part + 1) * width] = whitened[
                (row ^ step) * share + part
            ]
    lines = col_count // 2
    for step in range(lines):
        line = lax.rem(col // 2 + step, lines)
        for flip in range(2):
            to_cols[2 * step + flip][...] = whitened[2 * line + (lax.rem(col, 2) ^ flip)]


def make_spectra(record, fir_taps, bins, offsets, place, row_count, col_count):
    depth, channels = record.shape
    width = channels // col_count
    smem = pl.BlockSpec(memory_space=pltpu.SMEM)
    vmem = pl.BlockSpec(memory_space=pltpu.VMEM)
    outs = [jax.ShapeDtypeStruct((ROWS, channels // row_count), BF16)] * row_count
    outs += [jax.ShapeDtypeStruct((ROWS, width), BF16)] * col_count
    return pl.pallas_call(
        functools.partial(spectra_body, row_count, col_count),
        out_shape=outs,
        in_specs=[smem] * 4 + [pl.BlockSpec(memory_space=pl.ANY)],
        out_specs=[vmem] * len(outs),
        scratch_shapes=[
            pltpu.VMEM((col_count, depth, width), BF16),
            pltpu.VMEM((ROWS, depth + LANES), F32),
            pltpu.VMEM((depth // LANES * ROWS, 2 * LANES), F32),
            pltpu.VMEM((ROWS, depth), BF16),
            pltpu.VMEM((col_count, ROWS, width), BF16),
            pltpu.SemaphoreType.DMA((col_count,)),
        ],
        compiler_params=pltpu.CompilerParams(vmem_limit_bytes=48 * 2**20),
        name="spectra",
    )(place, offsets, bins, fir_taps, record)


def regroup_body(count, *refs):
    pieces = [ref[...].astype(F32) for ref in refs[:count]]
    for chunk in range(CHUNKS):
        rows = slice(chunk * GROUP, (chunk + 1) * GROUP)
        joined = jnp.concatenate([piece[rows] for piece in pieces], axis=0)
        per_call = CHUNKS // CALLS
        refs[count + chunk // per_call][chunk % per_call] = joined.astype(BF16)


def regroup(pieces):
    count, width = len(pieces), pieces[0].shape[1]
    out = jax.ShapeDtypeStruct((CHUNKS // CALLS, count * GROUP, width), BF16)
    vmem = pl.BlockSpec(memory_space=pltpu.VMEM)
    return pl.pallas_call(
        functools.partial(regroup_body, count),
        out_shape=[out] * CALLS,
        in_specs=[vmem] * count,
        out_specs=[vmem] * CALLS,
        name="regroup",
    )(*pieces)


def product_body(left_count, right_count, windows, *refs):
    lefts = refs[:left_count]
    rights = refs[left_count : left_count + right_count]
    out, turned, straight, crossed = refs[-4:]
    depth, width = straight.shape

    @pl.when(pl.program_id(1) == 0)
    def _():
        left = jnp.concatenate([ref[0] for ref in lefts], axis=0)
        turned[...] = left.T
        pieces = [ref[0].astype(F32) for ref in rights]
        right = jnp.concatenate(
            [
                piece[group * GROUP : (group + 1) * GROUP]
                for group in range(left_count)
                for piece in pieces
            ],
            axis=0,
        )
        straight[...] = right
        shaped = right.reshape(depth // GROUP, 2, CHUNK, width)
        swapped = jnp.stack([shaped[:, 1], -shaped[:, 0]], axis=1)
        crossed[...] = swapped.reshape(depth, width)

    row = lax.broadcasted_iota(jnp.int32, (depth, width), 0)
    wanted = row % CHUNK == pl.program_id(1)
    for part, held in enumerate((straight, crossed)):
        right = jnp.where(wanted, held[...], 0.0).astype(BF16)
        product = jnp.dot(turned[...], right, preferred_element_type=F32)
        out[0, part] = (product * (1.0 / windows)).astype(BF16)


def multiply(call, lefts, rights, windows, result):
    per_call, left_rows, height = lefts[0].shape
    right_rows, width = rights[0].shape[1:]
    depth = left_rows * len(lefts)
    in_specs = [pl.BlockSpec((1, left_rows, height), lambda q, f: (q, 0, 0))] * len(lefts)
    in_specs += [pl.BlockSpec((1, right_rows, width), lambda q, f: (q, 0, 0))] * len(rights)
    operands = [*lefts, *rights]
    aliases = {}
    if result is not None:
        aliases = {len(operands): 0}
        in_specs.append(pl.BlockSpec(memory_space=pl.ANY))
        operands.append(result)
    first = call * per_call * CHUNK
    return pl.pallas_call(
        functools.partial(product_body, len(lefts), len(rights), windows),
        out_shape=jax.ShapeDtypeStruct((F, 2, height, width), BF16),
        grid=(per_call, CHUNK),
        in_specs=in_specs,
        out_specs=pl.BlockSpec(
            (1, 2, height, width), lambda q, f: (first + q * CHUNK + f, 0, 0, 0)
        ),
        scratch_shapes=[
            pltpu.VMEM((height, depth), BF16),
            pltpu.VMEM((depth, width), F32),
            pltpu.VMEM((depth, width), F32),
        ],
        input_output_aliases=aliases,
        compiler_params=pltpu.CompilerParams(vmem_limit_bytes=48 * 2**20),
        cost_estimate=pl.CostEstimate(
            flops=2 * per_call * CHUNK * 2 * height * width * depth,
            bytes_accessed=per_call * CHUNK * 2 * height * width * 2,
            transcendentals=0,
        ),
        name="products",
    )(*operands)


def on_device(record, fir_taps, bins, offsets):
    row_count, col_count = lax.axis_size("row"), lax.axis_size("col")
    lines = col_count // 2
    windows = row_count * col_count * offsets.shape[0]
    place = jnp.stack([lax.axis_index("row"), lax.axis_index("col")]).astype(jnp.int32)

    def send(value, row_flip, line_step, core_flip):
        pairs = []
        for row in range(row_count):
            for col in range(col_count):
                line = (col // 2 + line_step) % lines
                target = (row ^ row_flip) * col_count + 2 * line + (col % 2 ^ core_flip)
                pairs.append((row * col_count + col, target))
        return lax.ppermute(value, AXES, pairs)

    spectra = make_spectra(record, fir_taps, bins, offsets, place, row_count, col_count)
    to_rows, to_cols = spectra[:row_count], spectra[row_count:]
    own_row = [to_rows[0]] + [send(to_rows[step], step, 0, 0) for step in range(1, row_count)]
    own_col = [to_cols[0]] + [
        send(to_cols[step], 0, step // 2, step % 2) for step in range(1, col_count)
    ]
    row_pieces = regroup(own_row)
    col_pieces = regroup(own_col)

    result = None
    for call in range(CALLS):
        held = row_pieces[call]
        lefts = []
        for step in range(lines):
            if step:
                held = send(held, 0, 1, 0)
            lefts += [held, send(held, 0, 0, 1)]
        rights = [col_pieces[call]] + [
            send(col_pieces[call], step, 0, 0) for step in range(1, row_count)
        ]
        result = multiply(call, lefts, rights, windows, result)
    return result


def solution(mesh):
    placed = (P(("row", "col"), None), P(), P(), P(("row", "col")))
    return jax.shard_map(
        on_device,
        mesh=mesh,
        in_specs=placed,
        out_specs=P(None, None, "row", "col"),
        check_vma=False,
    )
```

```python
import functools
import math

import jax
import jax.numpy as jnp
from jax import lax
from jax.experimental import pallas as pl
from jax.experimental.pallas import tpu as pltpu
from jax.sharding import PartitionSpec as P

F = 16
WL = 1280
TAPS = 101
SPAN = WL + TAPS - 1
LANES = 128
FLOOR = 0.5
CHUNK = 4
CHUNKS = F // CHUNK
GROUP = 2 * CHUNK
ROWS = 2 * F
CALLS = 2
WINDOW_GROUP = 2 * GROUP

AXES = ("row", "col")
BF16 = jnp.bfloat16
F32 = jnp.float32


def sine(x):
    square = x * x
    total = jnp.full_like(x, 1.0 / math.factorial(13))
    for order in (11, 9, 7, 5, 3, 1):
        sign = -1.0 if order % 4 == 3 else 1.0
        total = total * square + sign / math.factorial(order)
    return x * total


def analysis_rows(settings, pattern, stacked, kernel):
    depth = kernel.shape[1]
    blocks = depth // LANES
    times = lax.broadcasted_iota(jnp.int32, (1, WL), 1).astype(F32)
    row = lax.broadcasted_iota(jnp.int32, (ROWS, 1), 0)
    chosen = jnp.zeros((ROWS, 1), F32)
    for index in range(F):
        this = (row // GROUP == index // CHUNK) & (row % CHUNK == index % CHUNK)
        chosen = jnp.where(this, settings[TAPS + index], chosen)
    quarter = jnp.where(row % GROUP < CHUNK, 0.0, WL / 4.0)
    phase = chosen * times + quarter
    phase = phase - WL * jnp.floor((phase + 0.5) * (1.0 / WL))
    half = sine((phase - WL / 2.0) * (math.pi / WL))
    edge = times + 0.5
    taper = sine(jnp.minimum(edge, WL - edge) * (math.pi / WL))
    taper = taper * taper * (1.0 / math.sqrt(WL))
    pattern[:, :LANES] = jnp.zeros((ROWS, LANES), F32)
    pattern[:, LANES + WL :] = jnp.zeros((ROWS, depth - WL), F32)
    pattern[:, LANES : LANES + WL] = (2.0 * half * half - 1.0) * taper

    slack = depth - SPAN
    offset = settings[TAPS + F]
    lane = lax.broadcasted_iota(jnp.int32, (8, 2 * LANES), 1).astype(F32) - (slack - offset)
    filter_row = jnp.zeros((8, 2 * LANES), F32)
    for index in range(TAPS):
        filter_row = jnp.where(lane == index, settings[index], filter_row)
    filter_rows = jnp.concatenate([filter_row] * (LANES // 8), axis=0)
    band = pltpu.roll(filter_rows, 0, 1, stride=1, stride_axis=0)

    for block in range(blocks):
        stacked[block * ROWS : (block + 1) * ROWS, :] = pattern[
            :, block * LANES : (block + 2) * LANES
        ]
    filtered = lax.dot_general(
        stacked[...],
        band,
        (((1,), (1,)), ((), ())),
        precision=lax.Precision.HIGHEST,
        preferred_element_type=F32,
    )
    for block in range(blocks):
        kernel[:, block * LANES : (block + 1) * LANES] = filtered[
            block * ROWS : (block + 1) * ROWS
        ].astype(BF16)


def spectra_body(settings, record, whitened, samples, pattern, stacked, kernel, arrived):
    blocks, depth, width = samples.shape
    copies = []
    for block in range(blocks):
        copy = pltpu.make_async_copy(
            record.at[:, pl.ds(block * width, width)], samples.at[block], arrived.at[block]
        )
        copy.start()
        copies.append(copy)
    analysis_rows(settings, pattern, stacked, kernel)
    share = whitened.shape[2] // width
    for block in range(blocks):
        copies[block].wait()
        spectra = jnp.dot(kernel[...], samples[block], preferred_element_type=F32)
        shaped = spectra.reshape(CHUNKS, 2, CHUNK, width)
        real, imag = shaped[:, 0], shaped[:, 1]
        magnitude = jnp.sqrt(real * real + imag * imag)
        inverse = 1.0 / jnp.maximum(magnitude, FLOOR)
        scaled = (shaped * inverse[:, None]).reshape(ROWS, width)
        start = block % share * width
        whitened[block // share, :, start : start + width] = scaled.astype(BF16)


def make_spectra(record, settings, slices):
    depth, channels = record.shape
    blocks = 2 * slices
    width = channels // blocks
    return pl.pallas_call(
        spectra_body,
        out_shape=jax.ShapeDtypeStruct((slices, ROWS, channels // slices), BF16),
        in_specs=[pl.BlockSpec(memory_space=pltpu.SMEM), pl.BlockSpec(memory_space=pl.ANY)],
        out_specs=pl.BlockSpec(memory_space=pltpu.VMEM),
        scratch_shapes=[
            pltpu.VMEM((blocks, depth, width), BF16),
            pltpu.VMEM((ROWS, depth + LANES), F32),
            pltpu.VMEM((depth // LANES * ROWS, 2 * LANES), F32),
            pltpu.VMEM((ROWS, depth), BF16),
            pltpu.SemaphoreType.DMA((blocks,)),
        ],
        compiler_params=pltpu.CompilerParams(vmem_limit_bytes=24 * 2**20),
        name="spectra",
    )(settings, record)


def pair_body(own, other, *outs):
    row, col = lax.axis_index("row"), lax.axis_index("col")
    core = lax.rem(col, 2)
    place = jnp.where(core == 0, row, col // 2)
    for step, out in enumerate(outs):
        mine = own[place ^ step].astype(F32)
        theirs = other[place ^ step].astype(F32)
        first = jnp.where(core == 0, mine, theirs)
        second = jnp.where(core == 0, theirs, mine)
        pieces = []
        for chunk in range(CHUNKS):
            rows = slice(chunk * GROUP, (chunk + 1) * GROUP)
            pieces += [first[rows], second[rows]]
        out[...] = jnp.concatenate(pieces, axis=0).astype(BF16)


def pair_windows(own, other):
    slices, _, width = own.shape
    vmem = pl.BlockSpec(memory_space=pltpu.VMEM)
    return pl.pallas_call(
        pair_body,
        out_shape=[jax.ShapeDtypeStruct((2 * ROWS, width), BF16)] * slices,
        in_specs=[vmem] * 2,
        out_specs=[vmem] * slices,
        compiler_params=pltpu.CompilerParams(vmem_limit_bytes=8 * 2**20),
        name="pair_windows",
    )(own, other)


def regroup_body(count, *refs):
    per_call = CHUNKS // CALLS
    for chunk in range(CHUNKS):
        out = refs[count + chunk // per_call]
        for step in range(count):
            out[chunk % per_call, step * WINDOW_GROUP : (step + 1) * WINDOW_GROUP] = refs[step][
                chunk * WINDOW_GROUP : (chunk + 1) * WINDOW_GROUP
            ]


def regroup(pieces):
    count, width = len(pieces), pieces[0].shape[1]
    out = jax.ShapeDtypeStruct((CHUNKS // CALLS, count * WINDOW_GROUP, width), BF16)
    vmem = pl.BlockSpec(memory_space=pltpu.VMEM)
    return pl.pallas_call(
        functools.partial(regroup_body, count),
        out_shape=[out] * CALLS,
        in_specs=[vmem] * count,
        out_specs=[vmem] * CALLS,
        compiler_params=pltpu.CompilerParams(vmem_limit_bytes=8 * 2**20),
        name="regroup",
    )(*pieces)


def product_body(count, first, windows, *refs):
    held, swapped = refs[:count], refs[count : 2 * count]
    out, turned, straight, crossed, tiles, stored = refs[-6:]
    depth, width = straight.shape
    steps = tiles.shape[0]
    step = pl.program_id(0)
    chunk, index = step // CHUNK, lax.rem(step, CHUNK)
    core = lax.rem(lax.axis_index("col"), 2)

    def prepare(rows_of, cols_of, start):
        turned[...] = jnp.concatenate([ref[chunk] for ref in rows_of], axis=0).T
        pieces = [
            ref[chunk, group * WINDOW_GROUP : (group + 1) * WINDOW_GROUP, start : start + width]
            for group in range(count)
            for ref in cols_of
        ]
        right = jnp.concatenate(pieces, axis=0).astype(F32)
        straight[...] = right
        shaped = right.reshape(depth // GROUP, 2, CHUNK, width)
        crossed[...] = jnp.stack([shaped[:, 1], -shaped[:, 0]], axis=1).reshape(depth, width)

    pl.when((index == 0) & (core == 0))(functools.partial(prepare, held, swapped, 0))
    pl.when((index == 0) & (core == 1))(functools.partial(prepare, swapped, held, width))

    row = lax.broadcasted_iota(jnp.int32, (depth, width), 0)
    wanted = row % CHUNK == index
    for part, operand in enumerate((straight, crossed)):
        right = jnp.where(wanted, operand[...], 0.0).astype(BF16)
        product = jnp.dot(turned[...], right, preferred_element_type=F32)
        tiles[step, part] = (product * (1.0 / windows)).astype(BF16)
        pltpu.make_async_copy(
            tiles.at[step, part], out.at[first + step, part], stored.at[step, part]
        ).start()

    @pl.when(step == steps - 1)
    def _():
        for done in range(steps):
            for part in range(2):
                pltpu.make_async_copy(
                    tiles.at[done, part], out.at[first + done, part], stored.at[done, part]
                ).wait()


def multiply(call, held, swapped, windows, result):
    count = len(held)
    per_call, rows, height = held[0].shape
    depth, width = rows * count, height // 2
    steps = per_call * CHUNK
    vmem = pl.BlockSpec(memory_space=pltpu.VMEM)
    operands = [*held, *swapped]
    in_specs = [vmem] * len(operands)
    aliases = {}
    if result is not None:
        aliases = {len(operands): 0}
        in_specs.append(pl.BlockSpec(memory_space=pl.ANY))
        operands.append(result)
    return pl.pallas_call(
        functools.partial(product_body, count, call * steps, windows),
        out_shape=jax.ShapeDtypeStruct((F, 2, height, width), BF16),
        grid=(steps,),
        in_specs=in_specs,
        out_specs=pl.BlockSpec(memory_space=pl.ANY),
        scratch_shapes=[
            pltpu.VMEM((height, depth), BF16),
            pltpu.VMEM((depth, width), F32),
            pltpu.VMEM((depth, width), F32),
            pltpu.VMEM((steps, 2, height, width), BF16),
            pltpu.SemaphoreType.DMA((steps, 2)),
        ],
        input_output_aliases=aliases,
        compiler_params=pltpu.CompilerParams(vmem_limit_bytes=32 * 2**20),
        cost_estimate=pl.CostEstimate(
            flops=steps * 4 * height * width * depth,
            bytes_accessed=steps * 2 * height * width * 2,
            transcendentals=0,
        ),
        name="products",
    )(*operands)


def on_device(record, fir_taps, bins, offsets):
    row_count, col_count = lax.axis_size("row"), lax.axis_size("col")
    lines = col_count // 2
    windows = row_count * col_count

    def send(value, row_flip, line_flip, core_flip):
        pairs = []
        for row in range(row_count):
            for col in range(col_count):
                core, line = col % 2, col // 2
                target = 2 * (line ^ line_flip[core]) + (core ^ core_flip)
                pairs.append((row * col_count + col, (row ^ row_flip[core]) * col_count + target))
        return lax.ppermute(value, AXES, pairs)

    def swap(value):
        return send(value, (0, 0), (0, 0), 1)

    settings = jnp.concatenate([fir_taps, bins.astype(F32), offsets.astype(F32)])
    own = make_spectra(record, settings, row_count)
    to_send = pair_windows(own, swap(own))
    pieces = [to_send[0]]
    for step in range(1, row_count):
        pieces.append(send(to_send[step], (step, 0), (0, step), 0))
    started = regroup(pieces)

    result = None
    for call in range(CALLS):
        held = {0: started[call]}
        bit = row_count // 2
        while bit:
            for slot in list(held):
                held[slot ^ bit] = send(held[slot], (0, bit), (bit, 0), 0)
            bit //= 2
        ordered = [held[slot] for slot in range(row_count)]
        result = multiply(call, ordered, [swap(value) for value in ordered], windows, result)
    return result


def solution(mesh):
    placed = (P(("row", "col"), None), P(), P(), P(("row", "col")))
    return jax.shard_map(
        on_device,
        mesh=mesh,
        in_specs=placed,
        out_specs=P(None, None, "row", "col"),
        check_vma=False,
    )
```

```python
import functools
import math

import jax
import jax.numpy as jnp
from jax import lax
from jax.experimental import pallas as pl
from jax.experimental.pallas import tpu as pltpu
from jax.sharding import PartitionSpec as P

F = 16
WL = 1280
TAPS = 101
SPAN = WL + TAPS - 1
LANES = 128
FLOOR = 0.5
CHUNK = 4
CHUNKS = F // CHUNK
GROUP = 2 * CHUNK
ROWS = 2 * F
CALLS = 2
WINDOW_GROUP = 2 * GROUP

AXES = ("row", "col")
BF16 = jnp.bfloat16
F32 = jnp.float32


def sine(x):
    square = x * x
    total = jnp.full_like(x, 1.0 / math.factorial(13))
    for order in (11, 9, 7, 5, 3, 1):
        sign = -1.0 if order % 4 == 3 else 1.0
        total = total * square + sign / math.factorial(order)
    return x * total


def analysis_rows(taps, bins, offsets, pattern, stacked, kernel):
    depth = kernel.shape[1]
    blocks = depth // LANES
    times = lax.broadcasted_iota(jnp.int32, (1, WL), 1).astype(F32)
    row = lax.broadcasted_iota(jnp.int32, (ROWS, 1), 0)
    chosen = jnp.zeros((ROWS, 1), F32)
    for index in range(F):
        this = (row // GROUP == index // CHUNK) & (row % CHUNK == index % CHUNK)
        chosen = jnp.where(this, bins[index].astype(F32), chosen)
    quarter = jnp.where(row % GROUP < CHUNK, 0.0, WL / 4.0)
    phase = chosen * times + quarter
    phase = phase - WL * jnp.floor((phase + 0.5) * (1.0 / WL))
    half = sine((phase - WL / 2.0) * (math.pi / WL))
    edge = times + 0.5
    taper = sine(jnp.minimum(edge, WL - edge) * (math.pi / WL))
    taper = taper * taper * (1.0 / math.sqrt(WL))
    pattern[:, :LANES] = jnp.zeros((ROWS, LANES), F32)
    pattern[:, LANES + WL :] = jnp.zeros((ROWS, depth - WL), F32)
    pattern[:, LANES : LANES + WL] = (2.0 * half * half - 1.0) * taper

    slack = depth - SPAN
    lane = lax.broadcasted_iota(jnp.int32, (8, 2 * LANES), 1) - (slack - offsets[0])
    filter_row = jnp.zeros((8, 2 * LANES), F32)
    for index in range(TAPS):
        filter_row = jnp.where(lane == index, taps[index], filter_row)
    filter_rows = jnp.concatenate([filter_row] * (LANES // 8), axis=0)
    band = pltpu.roll(filter_rows, 0, 1, stride=1, stride_axis=0)

    for block in range(blocks):
        stacked[block * ROWS : (block + 1) * ROWS, :] = pattern[
            :, block * LANES : (block + 2) * LANES
        ]
    filtered = lax.dot_general(
        stacked[...],
        band,
        (((1,), (1,)), ((), ())),
        precision=lax.Precision.HIGHEST,
        preferred_element_type=F32,
    )
    for block in range(blocks):
        kernel[:, block * LANES : (block + 1) * LANES] = filtered[
            block * ROWS : (block + 1) * ROWS
        ].astype(BF16)


def spectra_body(fir_taps, bins, offsets, record, whitened, *scratch):
    samples, pattern, stacked, kernel, arrived, taps_held, bins_held, offsets_held, read = scratch
    blocks, depth, width = samples.shape
    small = []
    for index, pair in enumerate(
        ((fir_taps, taps_held), (bins, bins_held), (offsets, offsets_held))
    ):
        small.append(pltpu.make_async_copy(*pair, read.at[index]))
        small[-1].start()
    copies = []
    for block in range(blocks):
        copy = pltpu.make_async_copy(
            record.at[:, pl.ds(block * width, width)], samples.at[block], arrived.at[block]
        )
        copy.start()
        copies.append(copy)
    for copy in small:
        copy.wait()
    analysis_rows(taps_held, bins_held, offsets_held, pattern, stacked, kernel)
    share = whitened.shape[2] // width
    for block in range(blocks):
        copies[block].wait()
        spectra = jnp.dot(kernel[...], samples[block], preferred_element_type=F32)
        shaped = spectra.reshape(CHUNKS, 2, CHUNK, width)
        real, imag = shaped[:, 0], shaped[:, 1]
        magnitude = jnp.sqrt(real * real + imag * imag)
        inverse = 1.0 / jnp.maximum(magnitude, FLOOR)
        scaled = (shaped * inverse[:, None]).reshape(ROWS, width)
        start = block % share * width
        whitened[block // share, :, start : start + width] = scaled.astype(BF16)


def make_spectra(record, fir_taps, bins, offsets, slices):
    depth, channels = record.shape
    blocks = 2 * slices
    width = channels // blocks
    return pl.pallas_call(
        spectra_body,
        out_shape=jax.ShapeDtypeStruct((slices, ROWS, channels // slices), BF16),
        in_specs=[pl.BlockSpec(memory_space=pltpu.HBM)] * 4,
        out_specs=pl.BlockSpec(memory_space=pltpu.VMEM),
        scratch_shapes=[
            pltpu.VMEM((blocks, depth, width), BF16),
            pltpu.VMEM((ROWS, depth + LANES), F32),
            pltpu.VMEM((depth // LANES * ROWS, 2 * LANES), F32),
            pltpu.VMEM((ROWS, depth), BF16),
            pltpu.SemaphoreType.DMA((blocks,)),
            pltpu.SMEM(fir_taps.shape, F32),
            pltpu.SMEM(bins.shape, jnp.int32),
            pltpu.SMEM(offsets.shape, jnp.int32),
            pltpu.SemaphoreType.DMA((3,)),
        ],
        compiler_params=pltpu.CompilerParams(vmem_limit_bytes=56 * 2**20),
        name="spectra",
    )(fir_taps, bins, offsets, record)


def pair_body(own, other, *outs):
    row, col = lax.axis_index("row"), lax.axis_index("col")
    core = lax.rem(col, 2)
    place = jnp.where(core == 0, row, col // 2)
    for step, out in enumerate(outs):
        mine = own[place ^ step].astype(F32)
        theirs = other[place ^ step].astype(F32)
        first = jnp.where(core == 0, mine, theirs)
        second = jnp.where(core == 0, theirs, mine)
        pieces = []
        for chunk in range(CHUNKS):
            rows = slice(chunk * GROUP, (chunk + 1) * GROUP)
            pieces += [first[rows], second[rows]]
        out[...] = jnp.concatenate(pieces, axis=0).astype(BF16)


def pair_windows(own, other):
    slices, _, width = own.shape
    vmem = pl.BlockSpec(memory_space=pltpu.VMEM)
    return pl.pallas_call(
        pair_body,
        out_shape=[jax.ShapeDtypeStruct((2 * ROWS, width), BF16)] * slices,
        in_specs=[vmem] * 2,
        out_specs=[vmem] * slices,
        compiler_params=pltpu.CompilerParams(vmem_limit_bytes=8 * 2**20),
        name="pair_windows",
    )(own, other)


def regroup_body(call, count, *refs):
    out = refs[-1]
    for chunk in range(out.shape[0]):
        start = (call * out.shape[0] + chunk) * WINDOW_GROUP
        for step in range(count):
            out[chunk, step * WINDOW_GROUP : (step + 1) * WINDOW_GROUP] = refs[step][
                start : start + WINDOW_GROUP
            ]


def regroup(call, pieces, after):
    count, width = len(pieces), pieces[0].shape[1]
    vmem = pl.BlockSpec(memory_space=pltpu.VMEM)
    return pl.pallas_call(
        functools.partial(regroup_body, call, count),
        out_shape=jax.ShapeDtypeStruct((CHUNKS // CALLS, count * WINDOW_GROUP, width), BF16),
        in_specs=[vmem] * (count + len(after)),
        out_specs=vmem,
        compiler_params=pltpu.CompilerParams(vmem_limit_bytes=8 * 2**20),
        name="regroup",
    )(*pieces, *after)


def hold_body(value, after, out):
    out[...] = value[...]


def hold(value, after):
    vmem = pl.BlockSpec(memory_space=pltpu.VMEM)
    return pl.pallas_call(
        hold_body,
        out_shape=jax.ShapeDtypeStruct(value.shape, value.dtype),
        in_specs=[vmem, vmem],
        out_specs=vmem,
        compiler_params=pltpu.CompilerParams(vmem_limit_bytes=8 * 2**20),
        name="hold",
    )(value, after)


def product_body(count, first, windows, *refs):
    held, swapped = refs[:count], refs[count : 2 * count]
    out, finished, turned, right, tiles, stored = refs[-6:]
    depth, double = right.shape
    width = double // 2
    chunks = pl.num_programs(0)
    chunk = pl.program_id(0)
    core = lax.rem(lax.axis_index("col"), 2)

    def prepare(rows_of, cols_of, start):
        turned[...] = jnp.concatenate([ref[chunk] for ref in rows_of], axis=0).T
        pieces = [
            ref[chunk, group * WINDOW_GROUP : (group + 1) * WINDOW_GROUP, start : start + width]
            for group in range(count)
            for ref in cols_of
        ]
        straight = jnp.concatenate(pieces, axis=0).astype(F32)
        shaped = straight.reshape(depth // GROUP, 2, CHUNK, width)
        crossed = jnp.stack([shaped[:, 1], -shaped[:, 0]], axis=1).reshape(depth, width)
        right[:, :width] = straight
        right[:, width:] = crossed

    pl.when(core == 0)(functools.partial(prepare, held, swapped, 0))
    pl.when(core == 1)(functools.partial(prepare, swapped, held, width))

    def store(bin_index, part):
        return pltpu.make_async_copy(
            tiles.at[bin_index, part], out.at[first + bin_index, part], stored.at[bin_index, part]
        )

    row = lax.broadcasted_iota(jnp.int32, (depth, double), 0)
    for index in range(CHUNK):
        chosen = jnp.where(row % CHUNK == index, right[...], 0.0).astype(BF16)
        product = jnp.dot(turned[...], chosen, preferred_element_type=F32)
        for part in range(2):
            scaled = product[:, part * width : (part + 1) * width] * (1.0 / windows)
            tiles[chunk * CHUNK + index, part] = scaled.astype(BF16)
            store(chunk * CHUNK + index, part).start()

    @pl.when(chunk == chunks - 1)
    def _():
        for bin_index in range(tiles.shape[0]):
            for part in range(2):
                store(bin_index, part).wait()
        finished[...] = jnp.zeros_like(finished)


def multiply(call, held, swapped, windows, result, after):
    count = len(held)
    per_call, rows, height = held[0].shape
    depth, width = rows * count, height // 2
    steps = per_call * CHUNK
    vmem = pl.BlockSpec(memory_space=pltpu.VMEM)
    operands = [*held, *swapped, *after]
    in_specs = [vmem] * len(operands)
    aliases = {}
    if result is not None:
        aliases = {len(operands): 0}
        in_specs.append(pl.BlockSpec(memory_space=pl.ANY))
        operands.append(result)
    return pl.pallas_call(
        functools.partial(product_body, count, call * steps, windows),
        out_shape=[
            jax.ShapeDtypeStruct((F, 2, height, width), BF16),
            jax.ShapeDtypeStruct((8, LANES), F32),
        ],
        grid=(per_call,),
        in_specs=in_specs,
        out_specs=[pl.BlockSpec(memory_space=pl.ANY), vmem],
        scratch_shapes=[
            pltpu.VMEM((height, depth), BF16),
            pltpu.VMEM((depth, 2 * width), F32),
            pltpu.VMEM((steps, 2, height, width), BF16),
            pltpu.SemaphoreType.DMA((steps, 2)),
        ],
        input_output_aliases=aliases,
        compiler_params=pltpu.CompilerParams(vmem_limit_bytes=32 * 2**20),
        cost_estimate=pl.CostEstimate(
            flops=steps * 4 * height * width * depth,
            bytes_accessed=steps * 2 * height * width * 2,
            transcendentals=0,
        ),
        name="products",
    )(*operands)


def on_device(record, fir_taps, bins, offsets):
    row_count, col_count = lax.axis_size("row"), lax.axis_size("col")
    lines = col_count // 2
    windows = row_count * col_count

    def send(value, row_flip, line_flip, core_flip):
        pairs = []
        for row in range(row_count):
            for col in range(col_count):
                core, line = col % 2, col // 2
                target = 2 * (line ^ line_flip[core]) + (core ^ core_flip)
                pairs.append((row * col_count + col, (row ^ row_flip[core]) * col_count + target))
        return lax.ppermute(value, AXES, pairs)

    def swap(value):
        return send(value, (0, 0), (0, 0), 1)

    own = make_spectra(record, fir_taps, bins, offsets, row_count)
    to_send = pair_windows(own, swap(own))
    pieces = [to_send[0]]
    for step in range(1, row_count):
        pieces.append(send(to_send[step], (step, 0), (0, step), 0))

    bits = [row_count >> shift for shift in range(1, row_count.bit_length())]
    gathered, after = [], []
    for call in range(CALLS):
        held = {0: regroup(call, pieces, after)}
        for bit in bits:
            for slot in list(held):
                held[slot ^ bit] = send(held[slot], (0, bit), (bit, 0), 0)
        after = [held[bits[0]]]
        gathered.append(held)

    result, finished = None, None
    for call, held in enumerate(gathered):
        ordered = [held[slot] for slot in range(row_count)]
        last = row_count - 1
        if result is not None:
            ordered[last] = hold(ordered[last], finished)
        after = [gathered[call + 1][bits[0]]] if call + 1 < CALLS else []
        swapped = [swap(value) for value in ordered]
        result, finished = multiply(call, ordered, swapped, windows, result, after)
    return result


def solution(mesh):
    placed = (P(("row", "col"), None), P(), P(), P(("row", "col")))
    return jax.shard_map(
        on_device,
        mesh=mesh,
        in_specs=placed,
        out_specs=P(None, None, "row", "col"),
        check_vma=False,
    )
```

```python
import functools
import math

import jax
import jax.numpy as jnp
from jax import lax
from jax.experimental import pallas as pl
from jax.experimental.pallas import tpu as pltpu
from jax.sharding import PartitionSpec as P

F = 16
WL = 1280
TAPS = 101
SPAN = WL + TAPS - 1
LANES = 128
FLOOR = 0.5
CHUNK = 4
CHUNKS = F // CHUNK
GROUP = 2 * CHUNK
ROWS = 2 * F
WINDOW_GROUP = 2 * GROUP
GATES = {0: [1], 1: [1]}

AXES = ("row", "col")
BF16 = jnp.bfloat16
F32 = jnp.float32


def sine(x):
    square = x * x
    total = jnp.full_like(x, 1.0 / math.factorial(13))
    for order in (11, 9, 7, 5, 3, 1):
        sign = -1.0 if order % 4 == 3 else 1.0
        total = total * square + sign / math.factorial(order)
    return x * total


def analysis_rows(taps, bins, offsets, pattern, stacked, kernel):
    depth = kernel.shape[1]
    blocks = depth // LANES
    times = lax.broadcasted_iota(jnp.int32, (1, WL), 1).astype(F32)
    row = lax.broadcasted_iota(jnp.int32, (ROWS, 1), 0)
    chosen = jnp.zeros((ROWS, 1), F32)
    for index in range(F):
        this = (row // GROUP == index // CHUNK) & (row % CHUNK == index % CHUNK)
        chosen = jnp.where(this, bins[index].astype(F32), chosen)
    quarter = jnp.where(row % GROUP < CHUNK, 0.0, WL / 4.0)
    phase = chosen * times + quarter
    phase = phase - WL * jnp.floor((phase + 0.5) * (1.0 / WL))
    half = sine((phase - WL / 2.0) * (math.pi / WL))
    edge = times + 0.5
    taper = sine(jnp.minimum(edge, WL - edge) * (math.pi / WL))
    taper = taper * taper * (1.0 / math.sqrt(WL))
    pattern[:, :LANES] = jnp.zeros((ROWS, LANES), F32)
    pattern[:, LANES + WL :] = jnp.zeros((ROWS, depth - WL), F32)
    pattern[:, LANES : LANES + WL] = (2.0 * half * half - 1.0) * taper

    slack = depth - SPAN
    lane = lax.broadcasted_iota(jnp.int32, (8, 2 * LANES), 1) - (slack - offsets[0])
    filter_row = jnp.zeros((8, 2 * LANES), F32)
    for index in range(TAPS):
        filter_row = jnp.where(lane == index, taps[index], filter_row)
    filter_rows = jnp.concatenate([filter_row] * (LANES // 8), axis=0)
    band = pltpu.roll(filter_rows, 0, 1, stride=1, stride_axis=0)

    for block in range(blocks):
        stacked[block * ROWS : (block + 1) * ROWS, :] = pattern[
            :, block * LANES : (block + 2) * LANES
        ]
    filtered = lax.dot_general(
        stacked[...],
        band,
        (((1,), (1,)), ((), ())),
        precision=lax.Precision.HIGHEST,
        preferred_element_type=F32,
    )
    for block in range(blocks):
        kernel[:, block * LANES : (block + 1) * LANES] = filtered[
            block * ROWS : (block + 1) * ROWS
        ].astype(BF16)


def spectra_body(fir_taps, bins, offsets, record, whitened, *scratch):
    samples, pattern, stacked, kernel, arrived, taps_held, bins_held, offsets_held, read = scratch
    blocks, depth, width = samples.shape
    small = []
    for index, pair in enumerate(
        ((fir_taps, taps_held), (bins, bins_held), (offsets, offsets_held))
    ):
        small.append(pltpu.make_async_copy(*pair, read.at[index]))
        small[-1].start()
    copies = []
    for block in range(blocks):
        copy = pltpu.make_async_copy(
            record.at[:, pl.ds(block * width, width)], samples.at[block], arrived.at[block]
        )
        copy.start()
        copies.append(copy)
    for copy in small:
        copy.wait()
    analysis_rows(taps_held, bins_held, offsets_held, pattern, stacked, kernel)
    share = whitened.shape[2] // width
    for block in range(blocks):
        copies[block].wait()
        spectra = jnp.dot(kernel[...], samples[block], preferred_element_type=F32)
        shaped = spectra.reshape(CHUNKS, 2, CHUNK, width)
        real, imag = shaped[:, 0], shaped[:, 1]
        magnitude = jnp.sqrt(real * real + imag * imag)
        inverse = 1.0 / jnp.maximum(magnitude, FLOOR)
        scaled = (shaped * inverse[:, None]).reshape(ROWS, width)
        start = block % share * width
        whitened[block // share, :, start : start + width] = scaled.astype(BF16)


def make_spectra(record, fir_taps, bins, offsets, slices):
    depth, channels = record.shape
    blocks = 2 * slices
    width = channels // blocks
    return pl.pallas_call(
        spectra_body,
        out_shape=jax.ShapeDtypeStruct((slices, ROWS, channels // slices), BF16),
        in_specs=[pl.BlockSpec(memory_space=pltpu.HBM)] * 4,
        out_specs=pl.BlockSpec(memory_space=pltpu.VMEM),
        scratch_shapes=[
            pltpu.VMEM((blocks, depth, width), BF16),
            pltpu.VMEM((ROWS, depth + LANES), F32),
            pltpu.VMEM((depth // LANES * ROWS, 2 * LANES), F32),
            pltpu.VMEM((ROWS, depth), BF16),
            pltpu.SemaphoreType.DMA((blocks,)),
            pltpu.SMEM(fir_taps.shape, F32),
            pltpu.SMEM(bins.shape, jnp.int32),
            pltpu.SMEM(offsets.shape, jnp.int32),
            pltpu.SemaphoreType.DMA((3,)),
        ],
        compiler_params=pltpu.CompilerParams(vmem_limit_bytes=56 * 2**20),
        name="spectra",
    )(fir_taps, bins, offsets, record)


def pair_body(own, other, *outs):
    row, col = lax.axis_index("row"), lax.axis_index("col")
    core = lax.rem(col, 2)
    place = jnp.where(core == 0, row, col // 2)
    for step, out in enumerate(outs):
        mine = own[place ^ step].astype(F32)
        theirs = other[place ^ step].astype(F32)
        first = jnp.where(core == 0, mine, theirs)
        second = jnp.where(core == 0, theirs, mine)
        pieces = []
        for chunk in range(CHUNKS):
            rows = slice(chunk * GROUP, (chunk + 1) * GROUP)
            pieces += [first[rows], second[rows]]
        out[...] = jnp.concatenate(pieces, axis=0).astype(BF16)


def pair_windows(own, other):
    slices, _, width = own.shape
    vmem = pl.BlockSpec(memory_space=pltpu.VMEM)
    return pl.pallas_call(
        pair_body,
        out_shape=[jax.ShapeDtypeStruct((2 * ROWS, width), BF16)] * slices,
        in_specs=[vmem] * 2,
        out_specs=[vmem] * slices,
        compiler_params=pltpu.CompilerParams(vmem_limit_bytes=8 * 2**20),
        name="pair_windows",
    )(own, other)


def pack_body(*refs):
    for index, ref in enumerate(refs[:-1]):
        refs[-1][index] = ref[...]


def pack(values):
    vmem = pl.BlockSpec(memory_space=pltpu.VMEM)
    return pl.pallas_call(
        pack_body,
        out_shape=jax.ShapeDtypeStruct((len(values), *values[0].shape), BF16),
        in_specs=[vmem] * len(values),
        out_specs=vmem,
        compiler_params=pltpu.CompilerParams(vmem_limit_bytes=8 * 2**20),
        name="pack",
    )(*values)


def hold_body(value, *refs):
    refs[-1][...] = value[...]


def hold(value, after):
    vmem = pl.BlockSpec(memory_space=pltpu.VMEM)
    return pl.pallas_call(
        hold_body,
        out_shape=jax.ShapeDtypeStruct(value.shape, value.dtype),
        in_specs=[vmem] * (1 + len(after)),
        out_specs=vmem,
        compiler_params=pltpu.CompilerParams(vmem_limit_bytes=8 * 2**20),
        name="hold",
    )(value, *after)


def product_body(count, windows, *refs):
    held, swapped = refs[:count], refs[count : 2 * count]
    out, turned, right, tiles, stored = refs[2 * count :]
    depth, double = right.shape
    width = double // 2
    chunks = pl.num_programs(0)
    chunk = pl.program_id(0)
    core = lax.rem(lax.axis_index("col"), 2)

    def prepare(rows_of, cols_of, start):
        unit = pl.ds(pl.multiple_of(chunk * WINDOW_GROUP, WINDOW_GROUP), WINDOW_GROUP)
        lefts = [ref[line, unit] for line in range(count) for ref in rows_of]
        turned[...] = jnp.concatenate(lefts, axis=0).T
        columns = slice(start, start + width)
        rights = [ref[plane, unit, columns] for ref in cols_of for plane in range(count)]
        straight = jnp.concatenate(rights, axis=0).astype(F32)
        shaped = straight.reshape(depth // GROUP, 2, CHUNK, width)
        crossed = jnp.stack([shaped[:, 1], -shaped[:, 0]], axis=1).reshape(depth, width)
        right[:, :width] = straight
        right[:, width:] = crossed

    pl.when(core == 0)(functools.partial(prepare, held, swapped, 0))
    pl.when(core == 1)(functools.partial(prepare, swapped, held, width))

    def store(bin_index, part):
        return pltpu.make_async_copy(
            tiles.at[bin_index, part], out.at[bin_index, part], stored.at[bin_index, part]
        )

    row = lax.broadcasted_iota(jnp.int32, (depth, double), 0)
    for index in range(CHUNK):
        chosen = jnp.where(row % CHUNK == index, right[...], 0.0).astype(BF16)
        product = jnp.dot(turned[...], chosen, preferred_element_type=F32)
        for part in range(2):
            scaled = product[:, part * width : (part + 1) * width] * (1.0 / windows)
            tiles[chunk * CHUNK + index, part] = scaled.astype(BF16)
            store(chunk * CHUNK + index, part).start()

    @pl.when(chunk == chunks - 1)
    def _():
        for bin_index in range(tiles.shape[0]):
            for part in range(2):
                store(bin_index, part).wait()


def multiply(held, swapped, windows):
    count = len(held)
    height = held[0].shape[2]
    depth, width = count * count * WINDOW_GROUP, height // 2
    vmem = pl.BlockSpec(memory_space=pltpu.VMEM)
    return pl.pallas_call(
        functools.partial(product_body, count, windows),
        out_shape=jax.ShapeDtypeStruct((F, 2, height, width), BF16),
        grid=(CHUNKS,),
        in_specs=[vmem] * (2 * count),
        out_specs=pl.BlockSpec(memory_space=pl.ANY),
        scratch_shapes=[
            pltpu.VMEM((height, depth), BF16),
            pltpu.VMEM((depth, 2 * width), F32),
            pltpu.VMEM((F, 2, height, width), BF16),
            pltpu.SemaphoreType.DMA((F, 2)),
        ],
        compiler_params=pltpu.CompilerParams(vmem_limit_bytes=40 * 2**20),
        cost_estimate=pl.CostEstimate(
            flops=F * 4 * height * width * depth,
            bytes_accessed=F * 2 * height * width * 2,
            transcendentals=0,
        ),
        name="products",
    )(*held, *swapped)


def on_device(record, fir_taps, bins, offsets):
    row_count, col_count = lax.axis_size("row"), lax.axis_size("col")
    lines = col_count // 2
    windows = row_count * col_count

    def send(value, row_flip, line_flip, core_flip):
        pairs = []
        for row in range(row_count):
            for col in range(col_count):
                core, line = col % 2, col // 2
                target = 2 * (line ^ line_flip[core]) + (core ^ core_flip)
                pairs.append((row * col_count + col, (row ^ row_flip[core]) * col_count + target))
        return lax.ppermute(value, AXES, pairs)

    def swap(value):
        return send(value, (0, 0), (0, 0), 1)

    own = make_spectra(record, fir_taps, bins, offsets, row_count)
    to_send = pair_windows(hold(own, []), swap(own))
    pieces = [to_send[0]]
    for step in range(1, row_count):
        pieces.append(send(to_send[step], (step, 0), (0, step), 0))

    bits = [row_count >> shift for shift in range(1, row_count.bit_length())]
    units, early = [], []
    for step, piece in enumerate(pieces):
        if step == row_count - 1:
            piece = hold(piece, early)
        held = {0: piece}
        for bit in bits:
            for slot in list(held):
                held[slot ^ bit] = send(held[slot], (0, bit), (bit, 0), 0)
        if step in GATES:
            early += [held[bit] for bit in GATES[step]]
        units.append(pack([held[slot] for slot in range(row_count)]))
    return multiply(units, [swap(unit) for unit in units], windows)


def solution(mesh):
    placed = (P(("row", "col"), None), P(), P(), P(("row", "col")))
    return jax.shard_map(
        on_device,
        mesh=mesh,
        in_specs=placed,
        out_specs=P(None, None, "row", "col"),
        check_vma=False,
    )
```

```python
import functools
import math

import jax
import jax.numpy as jnp
from jax import lax
from jax.experimental import pallas as pl
from jax.experimental.pallas import tpu as pltpu
from jax.sharding import PartitionSpec as P

F = 16
WL = 1280
TAPS = 101
SPAN = WL + TAPS - 1
LANES = 128
FLOOR = 0.5
CHUNK = 4
CHUNKS = F // CHUNK
GROUP = 2 * CHUNK
ROWS = 2 * F
WINDOW_GROUP = 2 * GROUP

AXES = ("row", "col")
BF16 = jnp.bfloat16
F32 = jnp.float32


def sine(x):
    square = x * x
    total = jnp.full_like(x, 1.0 / math.factorial(13))
    for order in (11, 9, 7, 5, 3, 1):
        sign = -1.0 if order % 4 == 3 else 1.0
        total = total * square + sign / math.factorial(order)
    return x * total


def analysis_rows(taps, bins, offsets, pattern, stacked, kernel):
    depth = kernel.shape[1]
    blocks = depth // LANES
    times = lax.broadcasted_iota(jnp.int32, (1, WL), 1).astype(F32)
    row = lax.broadcasted_iota(jnp.int32, (ROWS, 1), 0)
    chosen = jnp.zeros((ROWS, 1), F32)
    for index in range(F):
        this = (row // GROUP == index // CHUNK) & (row % CHUNK == index % CHUNK)
        chosen = jnp.where(this, bins[index].astype(F32), chosen)
    quarter = jnp.where(row % GROUP < CHUNK, 0.0, WL / 4.0)
    phase = chosen * times + quarter
    phase = phase - WL * jnp.floor((phase + 0.5) * (1.0 / WL))
    half = sine((phase - WL / 2.0) * (math.pi / WL))
    edge = times + 0.5
    taper = sine(jnp.minimum(edge, WL - edge) * (math.pi / WL))
    taper = taper * taper * (1.0 / math.sqrt(WL))
    pattern[:, :LANES] = jnp.zeros((ROWS, LANES), F32)
    pattern[:, LANES + WL :] = jnp.zeros((ROWS, depth - WL), F32)
    pattern[:, LANES : LANES + WL] = (2.0 * half * half - 1.0) * taper

    slack = depth - SPAN
    lane = lax.broadcasted_iota(jnp.int32, (8, 2 * LANES), 1) - (slack - offsets[0])
    filter_row = jnp.zeros((8, 2 * LANES), F32)
    for index in range(TAPS):
        filter_row = jnp.where(lane == index, taps[index], filter_row)
    filter_rows = jnp.concatenate([filter_row] * (LANES // 8), axis=0)
    band = pltpu.roll(filter_rows, 0, 1, stride=1, stride_axis=0)

    for block in range(blocks):
        stacked[block * ROWS : (block + 1) * ROWS, :] = pattern[
            :, block * LANES : (block + 2) * LANES
        ]
    filtered = lax.dot_general(
        stacked[...],
        band,
        (((1,), (1,)), ((), ())),
        precision=lax.Precision.HIGHEST,
        preferred_element_type=F32,
    )
    for block in range(blocks):
        kernel[:, block * LANES : (block + 1) * LANES] = filtered[
            block * ROWS : (block + 1) * ROWS
        ].astype(BF16)


def spectra_body(fir_taps, bins, offsets, record, whitened, *scratch):
    samples, pattern, stacked, kernel, arrived, taps_held, bins_held, offsets_held, read = scratch
    blocks, depth, width = samples.shape
    small = []
    for index, pair in enumerate(
        ((fir_taps, taps_held), (bins, bins_held), (offsets, offsets_held))
    ):
        small.append(pltpu.make_async_copy(*pair, read.at[index]))
        small[-1].start()
    copies = []
    for block in range(blocks):
        copy = pltpu.make_async_copy(
            record.at[:, pl.ds(block * width, width)], samples.at[block], arrived.at[block]
        )
        copy.start()
        copies.append(copy)
    for copy in small:
        copy.wait()
    analysis_rows(taps_held, bins_held, offsets_held, pattern, stacked, kernel)
    share = whitened.shape[2] // width
    for block in range(blocks):
        copies[block].wait()
        spectra = jnp.dot(kernel[...], samples[block], preferred_element_type=F32)
        shaped = spectra.reshape(CHUNKS, 2, CHUNK, width)
        real, imag = shaped[:, 0], shaped[:, 1]
        magnitude = jnp.sqrt(real * real + imag * imag)
        inverse = 1.0 / jnp.maximum(magnitude, FLOOR)
        scaled = (shaped * inverse[:, None]).reshape(ROWS, width)
        start = block % share * width
        whitened[block // share, :, start : start + width] = scaled.astype(BF16)


def make_spectra(record, fir_taps, bins, offsets, slices):
    depth, channels = record.shape
    blocks = 2 * slices
    width = channels // blocks
    return pl.pallas_call(
        spectra_body,
        out_shape=jax.ShapeDtypeStruct((slices, ROWS, channels // slices), BF16),
        in_specs=[pl.BlockSpec(memory_space=pltpu.HBM)] * 4,
        out_specs=pl.BlockSpec(memory_space=pltpu.VMEM),
        scratch_shapes=[
            pltpu.VMEM((blocks, depth, width), BF16),
            pltpu.VMEM((ROWS, depth + LANES), F32),
            pltpu.VMEM((depth // LANES * ROWS, 2 * LANES), F32),
            pltpu.VMEM((ROWS, depth), BF16),
            pltpu.SemaphoreType.DMA((blocks,)),
            pltpu.SMEM(fir_taps.shape, F32),
            pltpu.SMEM(bins.shape, jnp.int32),
            pltpu.SMEM(offsets.shape, jnp.int32),
            pltpu.SemaphoreType.DMA((3,)),
        ],
        compiler_params=pltpu.CompilerParams(vmem_limit_bytes=56 * 2**20),
        name="spectra",
    )(fir_taps, bins, offsets, record)


def pair_body(own, other, *outs):
    row, col = lax.axis_index("row"), lax.axis_index("col")
    core = lax.rem(col, 2)
    place = jnp.where(core == 0, row, col // 2)
    for step, out in enumerate(outs):
        mine = own[place ^ step].astype(F32)
        theirs = other[place ^ step].astype(F32)
        first = jnp.where(core == 0, mine, theirs)
        second = jnp.where(core == 0, theirs, mine)
        pieces = []
        for chunk in range(CHUNKS):
            rows = slice(chunk * GROUP, (chunk + 1) * GROUP)
            pieces += [first[rows], second[rows]]
        out[...] = jnp.concatenate(pieces, axis=0).astype(BF16)


def pair_windows(own, other):
    slices, _, width = own.shape
    vmem = pl.BlockSpec(memory_space=pltpu.VMEM)
    return pl.pallas_call(
        pair_body,
        out_shape=[jax.ShapeDtypeStruct((2 * ROWS, width), BF16)] * slices,
        in_specs=[vmem] * 2,
        out_specs=[vmem] * slices,
        compiler_params=pltpu.CompilerParams(vmem_limit_bytes=8 * 2**20),
        cost_estimate=pl.CostEstimate(flops=1, bytes_accessed=1, transcendentals=0),
        name="pair_windows",
    )(own, other)


def pack_body(*refs):
    out, start = refs[-1], 0
    for ref in refs[:-1]:
        out[start : start + ref.shape[0]] = ref[...]
        start += ref.shape[0]


def pack(values):
    rows = sum(value.shape[0] for value in values)
    vmem = pl.BlockSpec(memory_space=pltpu.VMEM)
    return pl.pallas_call(
        pack_body,
        out_shape=jax.ShapeDtypeStruct((rows, *values[0].shape[1:]), BF16),
        in_specs=[vmem] * len(values),
        out_specs=vmem,
        compiler_params=pltpu.CompilerParams(vmem_limit_bytes=8 * 2**20),
        cost_estimate=pl.CostEstimate(flops=1, bytes_accessed=1, transcendentals=0),
        name="pack",
    )(*values)


def hold_body(value, *refs):
    refs[-1][...] = value[...]


def hold(value, after):
    vmem = pl.BlockSpec(memory_space=pltpu.VMEM)
    return pl.pallas_call(
        hold_body,
        out_shape=jax.ShapeDtypeStruct(value.shape, value.dtype),
        in_specs=[vmem] * (1 + len(after)),
        out_specs=vmem,
        compiler_params=pltpu.CompilerParams(vmem_limit_bytes=8 * 2**20),
        cost_estimate=pl.CostEstimate(flops=1, bytes_accessed=1, transcendentals=0),
        name="hold",
    )(value, *after)


def product_body(count, windows, places, *refs):
    arrays = len(refs) // 2 - 2
    held, swapped = refs[:arrays], refs[arrays : 2 * arrays]
    out, turned, right, tiles, stored = refs[2 * arrays :]
    depth, double = right.shape
    width = double // 2
    chunks = pl.num_programs(0)
    chunk = pl.program_id(0)
    core = lax.rem(lax.axis_index("col"), 2)

    def prepare(rows_of, cols_of, start):
        def take(arrays, first, second):
            array, start = places[first, second]
            base = pl.multiple_of(start + chunk * WINDOW_GROUP, WINDOW_GROUP)
            return arrays[array][pl.ds(base, WINDOW_GROUP), :]

        lefts = [take(rows_of, plane, line) for line in range(count) for plane in range(count)]
        turned[...] = jnp.concatenate(lefts, axis=0).T
        columns = slice(start, start + width)
        rights = [take(cols_of, line, plane) for line in range(count) for plane in range(count)]
        straight = jnp.concatenate(rights, axis=0)[:, columns].astype(F32)
        shaped = straight.reshape(depth // GROUP, 2, CHUNK, width)
        crossed = jnp.stack([shaped[:, 1], -shaped[:, 0]], axis=1).reshape(depth, width)
        right[:, :width] = straight
        right[:, width:] = crossed

    pl.when(core == 0)(functools.partial(prepare, held, swapped, 0))
    pl.when(core == 1)(functools.partial(prepare, swapped, held, width))

    def store(bin_index, part):
        return pltpu.make_async_copy(
            tiles.at[bin_index, part], out.at[bin_index, part], stored.at[bin_index, part]
        )

    row = lax.broadcasted_iota(jnp.int32, (depth, double), 0)
    for index in range(CHUNK):
        chosen = jnp.where(row % CHUNK == index, right[...], 0.0).astype(BF16)
        product = jnp.dot(turned[...], chosen, preferred_element_type=F32)
        for part in range(2):
            scaled = product[:, part * width : (part + 1) * width] * (1.0 / windows)
            tiles[chunk * CHUNK + index, part] = scaled.astype(BF16)
            store(chunk * CHUNK + index, part).start()

    @pl.when(chunk == chunks - 1)
    def _():
        for bin_index in range(tiles.shape[0]):
            for part in range(2):
                store(bin_index, part).wait()


def multiply(count, places, held, swapped, windows):
    height = held[0].shape[1]
    depth, width = count * count * WINDOW_GROUP, height // 2
    vmem = pl.BlockSpec(memory_space=pltpu.VMEM)
    return pl.pallas_call(
        functools.partial(product_body, count, windows, places),
        out_shape=jax.ShapeDtypeStruct((F, 2, height, width), BF16),
        grid=(CHUNKS,),
        in_specs=[vmem] * (2 * len(held)),
        out_specs=pl.BlockSpec(memory_space=pl.ANY),
        scratch_shapes=[
            pltpu.VMEM((height, depth), BF16),
            pltpu.VMEM((depth, 2 * width), F32),
            pltpu.VMEM((F, 2, height, width), BF16),
            pltpu.SemaphoreType.DMA((F, 2)),
        ],
        compiler_params=pltpu.CompilerParams(vmem_limit_bytes=40 * 2**20),
        cost_estimate=pl.CostEstimate(
            flops=F * 4 * height * width * depth,
            bytes_accessed=F * 2 * height * width * 2,
            transcendentals=0,
        ),
        name="products",
    )(*held, *swapped)


def on_device(record, fir_taps, bins, offsets):
    row_count, col_count = lax.axis_size("row"), lax.axis_size("col")
    lines = col_count // 2
    windows = row_count * col_count

    def send(value, row_flip, line_flip, core_flip):
        pairs = []
        for row in range(row_count):
            for col in range(col_count):
                core, line = col % 2, col // 2
                target = 2 * (line ^ line_flip[core]) + (core ^ core_flip)
                pairs.append((row * col_count + col, (row ^ row_flip[core]) * col_count + target))
        return lax.ppermute(value, AXES, pairs)

    def swap(value):
        return send(value, (0, 0), (0, 0), 1)

    own = make_spectra(record, fir_taps, bins, offsets, row_count)
    to_send = pair_windows(hold(own, []), swap(own))
    pieces = [to_send[0]]
    for step in range(1, row_count):
        pieces.append(send(to_send[step], (step, 0), (0, step), 0))

    bits = [row_count >> shift for shift in range(1, row_count.bit_length())]
    packs, places, early = [], {}, []
    for step, piece in enumerate(pieces):
        if step == row_count - 1:
            piece = hold(piece, early[:2])
        held = {0: piece}
        for bit in bits:
            for slot in list(held):
                held[slot ^ bit] = send(held[slot], (0, bit), (bit, 0), 0)
        early.append(held[1])
        for order, slot in enumerate(held):
            places[step, slot] = (step, order * 2 * ROWS)
        packs.append(pack(list(held.values())))
    return multiply(row_count, places, packs, [swap(value) for value in packs], windows)


def solution(mesh):
    placed = (P(("row", "col"), None), P(), P(), P(("row", "col")))
    return jax.shard_map(
        on_device,
        mesh=mesh,
        in_specs=placed,
        out_specs=P(None, None, "row", "col"),
        check_vma=False,
    )
```

```python
import functools
import math

import jax
import jax.numpy as jnp
from jax import lax
from jax.experimental import pallas as pl
from jax.experimental.pallas import tpu as pltpu
from jax.sharding import PartitionSpec as P

F = 16
WL = 1280
TAPS = 101
SPAN = WL + TAPS - 1
LANES = 128
FLOOR = 0.5
CHUNK = 4
CHUNKS = F // CHUNK
GROUP = 2 * CHUNK
ROWS = 2 * F
WINDOW_GROUP = 2 * GROUP

AXES = ("row", "col")
BF16 = jnp.bfloat16
F32 = jnp.float32


def sine(x):
    square = x * x
    total = jnp.full_like(x, 1.0 / math.factorial(13))
    for order in (11, 9, 7, 5, 3, 1):
        sign = -1.0 if order % 4 == 3 else 1.0
        total = total * square + sign / math.factorial(order)
    return x * total


def analysis_rows(taps, bins, offsets, pattern, stacked, kernel):
    depth = kernel.shape[1]
    blocks = depth // LANES
    times = lax.broadcasted_iota(jnp.int32, (1, WL), 1).astype(F32)
    row = lax.broadcasted_iota(jnp.int32, (ROWS, 1), 0)
    chosen = jnp.zeros((ROWS, 1), F32)
    for index in range(F):
        this = (row // GROUP == index // CHUNK) & (row % CHUNK == index % CHUNK)
        chosen = jnp.where(this, bins[index].astype(F32), chosen)
    quarter = jnp.where(row % GROUP < CHUNK, 0.0, WL / 4.0)
    phase = chosen * times + quarter
    phase = phase - WL * jnp.floor((phase + 0.5) * (1.0 / WL))
    half = sine((phase - WL / 2.0) * (math.pi / WL))
    edge = times + 0.5
    taper = sine(jnp.minimum(edge, WL - edge) * (math.pi / WL))
    taper = taper * taper * (1.0 / math.sqrt(WL))
    pattern[:, :LANES] = jnp.zeros((ROWS, LANES), F32)
    pattern[:, LANES + WL :] = jnp.zeros((ROWS, depth - WL), F32)
    pattern[:, LANES : LANES + WL] = (2.0 * half * half - 1.0) * taper

    slack = depth - SPAN
    lane = lax.broadcasted_iota(jnp.int32, (8, 2 * LANES), 1) - (slack - offsets[0])
    filter_row = jnp.zeros((8, 2 * LANES), F32)
    for index in range(TAPS):
        filter_row = jnp.where(lane == index, taps[index], filter_row)
    filter_rows = jnp.concatenate([filter_row] * (LANES // 8), axis=0)
    band = pltpu.roll(filter_rows, 0, 1, stride=1, stride_axis=0)

    for block in range(blocks):
        stacked[block * ROWS : (block + 1) * ROWS, :] = pattern[
            :, block * LANES : (block + 2) * LANES
        ]
    filtered = lax.dot_general(
        stacked[...],
        band,
        (((1,), (1,)), ((), ())),
        precision=lax.Precision.HIGHEST,
        preferred_element_type=F32,
    )
    for block in range(blocks):
        kernel[:, block * LANES : (block + 1) * LANES] = filtered[
            block * ROWS : (block + 1) * ROWS
        ].astype(BF16)


def spectra_body(fir_taps, bins, offsets, record, whitened, *scratch):
    samples, pattern, stacked, kernel, arrived, taps_held, bins_held, offsets_held, read = scratch
    blocks, depth, width = samples.shape
    small = []
    for index, pair in enumerate(
        ((fir_taps, taps_held), (bins, bins_held), (offsets, offsets_held))
    ):
        small.append(pltpu.make_async_copy(*pair, read.at[index]))
        small[-1].start()
    copies = []
    for block in range(blocks):
        copy = pltpu.make_async_copy(
            record.at[:, pl.ds(block * width, width)], samples.at[block], arrived.at[block]
        )
        copy.start()
        copies.append(copy)
    for copy in small:
        copy.wait()
    analysis_rows(taps_held, bins_held, offsets_held, pattern, stacked, kernel)
    share = whitened.shape[2] // width
    for block in range(blocks):
        copies[block].wait()
        spectra = jnp.dot(kernel[...], samples[block], preferred_element_type=F32)
        shaped = spectra.reshape(CHUNKS, 2, CHUNK, width)
        real, imag = shaped[:, 0], shaped[:, 1]
        magnitude = jnp.sqrt(real * real + imag * imag)
        inverse = 1.0 / jnp.maximum(magnitude, FLOOR)
        scaled = (shaped * inverse[:, None]).reshape(ROWS, width)
        start = block % share * width
        whitened[block // share, :, start : start + width] = scaled.astype(BF16)


def make_spectra(record, fir_taps, bins, offsets, slices):
    depth, channels = record.shape
    blocks = 2 * slices
    width = channels // blocks
    return pl.pallas_call(
        spectra_body,
        out_shape=jax.ShapeDtypeStruct((slices, ROWS, channels // slices), BF16),
        in_specs=[pl.BlockSpec(memory_space=pltpu.HBM)] * 4,
        out_specs=pl.BlockSpec(memory_space=pltpu.VMEM),
        scratch_shapes=[
            pltpu.VMEM((blocks, depth, width), BF16),
            pltpu.VMEM((ROWS, depth + LANES), F32),
            pltpu.VMEM((depth // LANES * ROWS, 2 * LANES), F32),
            pltpu.VMEM((ROWS, depth), BF16),
            pltpu.SemaphoreType.DMA((blocks,)),
            pltpu.SMEM(fir_taps.shape, F32),
            pltpu.SMEM(bins.shape, jnp.int32),
            pltpu.SMEM(offsets.shape, jnp.int32),
            pltpu.SemaphoreType.DMA((3,)),
        ],
        compiler_params=pltpu.CompilerParams(vmem_limit_bytes=56 * 2**20),
        name="spectra",
    )(fir_taps, bins, offsets, record)


def pair_body(own, other, *outs):
    row, col = lax.axis_index("row"), lax.axis_index("col")
    core = lax.rem(col, 2)
    place = jnp.where(core == 0, row, col // 2)
    for step, out in enumerate(outs):
        mine = own[place ^ step].astype(F32)
        theirs = other[place ^ step].astype(F32)
        first = jnp.where(core == 0, mine, theirs)
        second = jnp.where(core == 0, theirs, mine)
        pieces = []
        for chunk in range(CHUNKS):
            rows = slice(chunk * GROUP, (chunk + 1) * GROUP)
            pieces += [first[rows], second[rows]]
        out[...] = jnp.concatenate(pieces, axis=0).astype(BF16)


def pair_windows(own, other):
    slices, _, width = own.shape
    vmem = pl.BlockSpec(memory_space=pltpu.VMEM)
    return pl.pallas_call(
        pair_body,
        out_shape=[jax.ShapeDtypeStruct((2 * ROWS, width), BF16)] * slices,
        in_specs=[vmem] * 2,
        out_specs=[vmem] * slices,
        compiler_params=pltpu.CompilerParams(vmem_limit_bytes=8 * 2**20),
        cost_estimate=pl.CostEstimate(flops=1, bytes_accessed=1, transcendentals=0),
        name="pair_windows",
    )(own, other)


def pack_body(*refs):
    out, start = refs[-1], 0
    for ref in refs[:-1]:
        out[start : start + ref.shape[0]] = ref[...]
        start += ref.shape[0]


def pack(values):
    rows = sum(value.shape[0] for value in values)
    vmem = pl.BlockSpec(memory_space=pltpu.VMEM)
    return pl.pallas_call(
        pack_body,
        out_shape=jax.ShapeDtypeStruct((rows, *values[0].shape[1:]), BF16),
        in_specs=[vmem] * len(values),
        out_specs=vmem,
        compiler_params=pltpu.CompilerParams(vmem_limit_bytes=8 * 2**20),
        cost_estimate=pl.CostEstimate(flops=1, bytes_accessed=1, transcendentals=0),
        name="pack",
    )(*values)


def hold_body(value, *refs):
    refs[-1][...] = value[...]


def hold(value, after):
    vmem = pl.BlockSpec(memory_space=pltpu.VMEM)
    return pl.pallas_call(
        hold_body,
        out_shape=jax.ShapeDtypeStruct(value.shape, value.dtype),
        in_specs=[vmem] * (1 + len(after)),
        out_specs=vmem,
        compiler_params=pltpu.CompilerParams(vmem_limit_bytes=8 * 2**20),
        cost_estimate=pl.CostEstimate(flops=1, bytes_accessed=1, transcendentals=0),
        name="hold",
    )(value, *after)


def product_body(count, windows, places, *refs):
    arrays = len(refs) // 2 - 2
    held, swapped = refs[:arrays], refs[arrays : 2 * arrays]
    out, turned, right, tiles, stored = refs[2 * arrays :]
    depth, double = right.shape
    width = double // 2
    chunks = pl.num_programs(0)
    chunk = pl.program_id(0)
    core = lax.rem(lax.axis_index("col"), 2)

    def prepare(rows_of, cols_of, start):
        def take(arrays, first, second):
            array, start = places[first, second]
            base = pl.multiple_of(start + chunk * WINDOW_GROUP, WINDOW_GROUP)
            return arrays[array][pl.ds(base, WINDOW_GROUP), :]

        lefts = [take(rows_of, plane, line) for line in range(count) for plane in range(count)]
        turned[...] = jnp.concatenate(lefts, axis=0).T
        columns = slice(start, start + width)
        rights = [take(cols_of, line, plane) for line in range(count) for plane in range(count)]
        straight = jnp.concatenate(rights, axis=0)[:, columns].astype(F32)
        shaped = straight.reshape(depth // GROUP, 2, CHUNK, width)
        crossed = jnp.stack([shaped[:, 1], -shaped[:, 0]], axis=1).reshape(depth, width)
        right[:, :width] = straight
        right[:, width:] = crossed

    pl.when(core == 0)(functools.partial(prepare, held, swapped, 0))
    pl.when(core == 1)(functools.partial(prepare, swapped, held, width))

    def store(bin_index, part):
        return pltpu.make_async_copy(
            tiles.at[bin_index, part], out.at[bin_index, part], stored.at[bin_index, part]
        )

    row = lax.broadcasted_iota(jnp.int32, (depth, double), 0)
    for index in range(CHUNK):
        chosen = jnp.where(row % CHUNK == index, right[...], 0.0).astype(BF16)
        product = jnp.dot(turned[...], chosen, preferred_element_type=F32)
        for part in range(2):
            scaled = product[:, part * width : (part + 1) * width] * (1.0 / windows)
            tiles[chunk * CHUNK + index, part] = scaled.astype(BF16)
            store(chunk * CHUNK + index, part).start()

    @pl.when(chunk == chunks - 1)
    def _():
        for bin_index in range(tiles.shape[0]):
            for part in range(2):
                store(bin_index, part).wait()


def multiply(count, places, held, swapped, windows):
    height = held[0].shape[1]
    depth, width = count * count * WINDOW_GROUP, height // 2
    vmem = pl.BlockSpec(memory_space=pltpu.VMEM)
    return pl.pallas_call(
        functools.partial(product_body, count, windows, places),
        out_shape=jax.ShapeDtypeStruct((F, 2, height, width), BF16),
        grid=(CHUNKS,),
        in_specs=[vmem] * (2 * len(held)),
        out_specs=pl.BlockSpec(memory_space=pl.ANY),
        scratch_shapes=[
            pltpu.VMEM((height, depth), BF16),
            pltpu.VMEM((depth, 2 * width), F32),
            pltpu.VMEM((F, 2, height, width), BF16),
            pltpu.SemaphoreType.DMA((F, 2)),
        ],
        compiler_params=pltpu.CompilerParams(vmem_limit_bytes=40 * 2**20),
        cost_estimate=pl.CostEstimate(
            flops=F * 4 * height * width * depth,
            bytes_accessed=F * 2 * height * width * 2,
            transcendentals=0,
        ),
        name="products",
    )(*held, *swapped)


def on_device(record, fir_taps, bins, offsets):
    row_count, col_count = lax.axis_size("row"), lax.axis_size("col")
    lines = col_count // 2
    windows = row_count * col_count

    def send(value, row_flip, line_flip, core_flip):
        pairs = []
        for row in range(row_count):
            for col in range(col_count):
                core, line = col % 2, col // 2
                target = 2 * (line ^ line_flip[core]) + (core ^ core_flip)
                pairs.append((row * col_count + col, (row ^ row_flip[core]) * col_count + target))
        return lax.ppermute(value, AXES, pairs)

    def swap(value):
        return send(value, (0, 0), (0, 0), 1)

    own = make_spectra(record, fir_taps, bins, offsets, row_count)
    to_send = pair_windows(hold(own, []), swap(own))
    turns = [0, *reversed(range(1, row_count))]
    pieces = {0: to_send[0]}
    for step in turns[1:]:
        pieces[step] = send(to_send[step], (step, 0), (0, step), 0)

    bits = [row_count >> shift for shift in range(1, row_count.bit_length())]
    packs, places, early = [], {}, []
    for step, piece in pieces.items():
        if step == turns[-1]:
            piece = hold(piece, early[:2])
        held = {0: piece}
        for bit in bits:
            for slot in list(held):
                held[slot ^ bit] = send(held[slot], (0, bit), (bit, 0), 0)
        early.append(held[1])
        for order, slot in enumerate(held):
            places[step, slot] = (len(packs), order * 2 * ROWS)
        packs.append(pack(list(held.values())))
    return multiply(row_count, places, packs, [swap(value) for value in packs], windows)


def solution(mesh):
    placed = (P(("row", "col"), None), P(), P(), P(("row", "col")))
    return jax.shard_map(
        on_device,
        mesh=mesh,
        in_specs=placed,
        out_specs=P(None, None, "row", "col"),
        check_vma=False,
    )
```

```python
import functools
import math

import jax
import jax.numpy as jnp
from jax import lax
from jax.experimental import pallas as pl
from jax.experimental.pallas import tpu as pltpu
from jax.sharding import PartitionSpec as P

F = 16
WL = 1280
TAPS = 101
SPAN = WL + TAPS - 1
LANES = 128
FLOOR = 0.5
CHUNK = 4
CHUNKS = F // CHUNK
GROUP = 2 * CHUNK
ROWS = 2 * F
WINDOW_GROUP = 2 * GROUP

AXES = ("row", "col")
BF16 = jnp.bfloat16
F32 = jnp.float32


def sine(x):
    square = x * x
    total = jnp.full_like(x, 1.0 / math.factorial(13))
    for order in (11, 9, 7, 5, 3, 1):
        sign = -1.0 if order % 4 == 3 else 1.0
        total = total * square + sign / math.factorial(order)
    return x * total


def analysis_rows(taps, bins, offsets, pattern, stacked, kernel):
    depth = kernel.shape[1]
    blocks = depth // LANES
    times = lax.broadcasted_iota(jnp.int32, (1, WL), 1).astype(F32)
    row = lax.broadcasted_iota(jnp.int32, (ROWS, 1), 0)
    chosen = jnp.zeros((ROWS, 1), F32)
    for index in range(F):
        this = (row // GROUP == index // CHUNK) & (row % CHUNK == index % CHUNK)
        chosen = jnp.where(this, bins[index].astype(F32), chosen)
    quarter = jnp.where(row % GROUP < CHUNK, 0.0, WL / 4.0)
    phase = chosen * times + quarter
    phase = phase - WL * jnp.floor((phase + 0.5) * (1.0 / WL))
    half = sine((phase - WL / 2.0) * (math.pi / WL))
    edge = times + 0.5
    taper = sine(jnp.minimum(edge, WL - edge) * (math.pi / WL))
    taper = taper * taper * (1.0 / math.sqrt(WL))
    pattern[:, :LANES] = jnp.zeros((ROWS, LANES), F32)
    pattern[:, LANES + WL :] = jnp.zeros((ROWS, depth - WL), F32)
    pattern[:, LANES : LANES + WL] = (2.0 * half * half - 1.0) * taper

    slack = depth - SPAN
    lane = lax.broadcasted_iota(jnp.int32, (8, 2 * LANES), 1) - (slack - offsets[0])
    filter_row = jnp.zeros((8, 2 * LANES), F32)
    for index in range(TAPS):
        filter_row = jnp.where(lane == index, taps[index], filter_row)
    filter_rows = jnp.concatenate([filter_row] * (LANES // 8), axis=0)
    band = pltpu.roll(filter_rows, 0, 1, stride=1, stride_axis=0)

    for block in range(blocks):
        stacked[block * ROWS : (block + 1) * ROWS, :] = pattern[
            :, block * LANES : (block + 2) * LANES
        ]
    filtered = lax.dot_general(
        stacked[...],
        band,
        (((1,), (1,)), ((), ())),
        precision=lax.Precision.HIGHEST,
        preferred_element_type=F32,
    )
    for block in range(blocks):
        kernel[:, block * LANES : (block + 1) * LANES] = filtered[
            block * ROWS : (block + 1) * ROWS
        ].astype(BF16)


def spectra_body(fir_taps, bins, offsets, record, whitened, *scratch):
    samples, pattern, stacked, kernel, arrived, taps_held, bins_held, offsets_held, read = scratch
    blocks, depth, width = samples.shape
    small = []
    for index, pair in enumerate(
        ((fir_taps, taps_held), (bins, bins_held), (offsets, offsets_held))
    ):
        small.append(pltpu.make_async_copy(*pair, read.at[index]))
        small[-1].start()
    copies = []
    for block in range(blocks):
        copy = pltpu.make_async_copy(
            record.at[:, pl.ds(block * width, width)], samples.at[block], arrived.at[block]
        )
        copy.start()
        copies.append(copy)
    for copy in small:
        copy.wait()
    analysis_rows(taps_held, bins_held, offsets_held, pattern, stacked, kernel)
    share = whitened.shape[2] // width
    for block in range(blocks):
        copies[block].wait()
        spectra = jnp.dot(kernel[...], samples[block], preferred_element_type=F32)
        shaped = spectra.reshape(CHUNKS, 2, CHUNK, width)
        real, imag = shaped[:, 0], shaped[:, 1]
        magnitude = jnp.sqrt(real * real + imag * imag)
        inverse = 1.0 / jnp.maximum(magnitude, FLOOR)
        scaled = (shaped * inverse[:, None]).reshape(ROWS, width)
        start = block % share * width
        whitened[block // share, :, start : start + width] = scaled.astype(BF16)


def make_spectra(record, fir_taps, bins, offsets, slices):
    depth, channels = record.shape
    blocks = 2 * slices
    width = channels // blocks
    return pl.pallas_call(
        spectra_body,
        out_shape=jax.ShapeDtypeStruct((slices, ROWS, channels // slices), BF16),
        in_specs=[pl.BlockSpec(memory_space=pltpu.HBM)] * 4,
        out_specs=pl.BlockSpec(memory_space=pltpu.VMEM),
        scratch_shapes=[
            pltpu.VMEM((blocks, depth, width), BF16),
            pltpu.VMEM((ROWS, depth + LANES), F32),
            pltpu.VMEM((depth // LANES * ROWS, 2 * LANES), F32),
            pltpu.VMEM((ROWS, depth), BF16),
            pltpu.SemaphoreType.DMA((blocks,)),
            pltpu.SMEM(fir_taps.shape, F32),
            pltpu.SMEM(bins.shape, jnp.int32),
            pltpu.SMEM(offsets.shape, jnp.int32),
            pltpu.SemaphoreType.DMA((3,)),
        ],
        compiler_params=pltpu.CompilerParams(vmem_limit_bytes=56 * 2**20),
        name="spectra",
    )(fir_taps, bins, offsets, record)


def pair_body(own, other, *outs):
    row, col = lax.axis_index("row"), lax.axis_index("col")
    core = lax.rem(col, 2)
    place = jnp.where(core == 0, row, col // 2)
    for step, out in enumerate(outs):
        mine = own[place ^ step].astype(F32)
        theirs = other[place ^ step].astype(F32)
        first = jnp.where(core == 0, mine, theirs)
        second = jnp.where(core == 0, theirs, mine)
        pieces = []
        for chunk in range(CHUNKS):
            rows = slice(chunk * GROUP, (chunk + 1) * GROUP)
            pieces += [first[rows], second[rows]]
        out[...] = jnp.concatenate(pieces, axis=0).astype(BF16)


def pair_windows(own, other):
    slices, _, width = own.shape
    vmem = pl.BlockSpec(memory_space=pltpu.VMEM)
    return pl.pallas_call(
        pair_body,
        out_shape=[jax.ShapeDtypeStruct((2 * ROWS, width), BF16)] * slices,
        in_specs=[vmem] * 2,
        out_specs=[vmem] * slices,
        compiler_params=pltpu.CompilerParams(vmem_limit_bytes=8 * 2**20),
        cost_estimate=pl.CostEstimate(flops=1, bytes_accessed=1, transcendentals=0),
        name="pair_windows",
    )(own, other)


def pack_body(*refs):
    out, start = refs[-1], 0
    for ref in refs[:-1]:
        out[start : start + ref.shape[0]] = ref[...]
        start += ref.shape[0]


def pack(values):
    rows = sum(value.shape[0] for value in values)
    vmem = pl.BlockSpec(memory_space=pltpu.VMEM)
    return pl.pallas_call(
        pack_body,
        out_shape=jax.ShapeDtypeStruct((rows, *values[0].shape[1:]), BF16),
        in_specs=[vmem] * len(values),
        out_specs=vmem,
        compiler_params=pltpu.CompilerParams(vmem_limit_bytes=8 * 2**20),
        cost_estimate=pl.CostEstimate(flops=1, bytes_accessed=1, transcendentals=0),
        name="pack",
    )(*values)


def hold_body(value, *refs):
    refs[-1][...] = value[...]


def hold(value, after):
    vmem = pl.BlockSpec(memory_space=pltpu.VMEM)
    return pl.pallas_call(
        hold_body,
        out_shape=jax.ShapeDtypeStruct(value.shape, value.dtype),
        in_specs=[vmem] * (1 + len(after)),
        out_specs=vmem,
        compiler_params=pltpu.CompilerParams(vmem_limit_bytes=8 * 2**20),
        cost_estimate=pl.CostEstimate(flops=1, bytes_accessed=1, transcendentals=0),
        name="hold",
    )(value, *after)


def product_body(count, windows, places, *refs):
    arrays = len(refs) // 2 - 2
    held, swapped = refs[:arrays], refs[arrays : 2 * arrays]
    out, turned, right, tiles, stored = refs[2 * arrays :]
    depth, double = right.shape
    width = double // 2
    chunks = pl.num_programs(0)
    chunk = pl.program_id(0)
    core = lax.rem(lax.axis_index("col"), 2)

    def prepare(rows_of, cols_of, start):
        def take(arrays, first, second):
            array, start = places[first, second]
            base = pl.multiple_of(start + chunk * WINDOW_GROUP, WINDOW_GROUP)
            return arrays[array][pl.ds(base, WINDOW_GROUP), :]

        lefts = [take(rows_of, plane, line) for line in range(count) for plane in range(count)]
        turned[...] = jnp.concatenate(lefts, axis=0).T
        columns = slice(start, start + width)
        rights = [take(cols_of, line, plane) for line in range(count) for plane in range(count)]
        straight = jnp.concatenate(rights, axis=0)[:, columns].astype(F32)
        shaped = straight.reshape(depth // GROUP, 2, CHUNK, width)
        crossed = jnp.stack([shaped[:, 1], -shaped[:, 0]], axis=1).reshape(depth, width)
        right[:, :width] = straight
        right[:, width:] = crossed

    pl.when(core == 0)(functools.partial(prepare, held, swapped, 0))
    pl.when(core == 1)(functools.partial(prepare, swapped, held, width))

    def store(bin_index, part):
        return pltpu.make_async_copy(
            tiles.at[bin_index, part], out.at[bin_index, part], stored.at[bin_index, part]
        )

    row = lax.broadcasted_iota(jnp.int32, (depth, double), 0)
    for index in range(CHUNK):
        chosen = jnp.where(row % CHUNK == index, right[...], 0.0).astype(BF16)
        product = jnp.dot(turned[...], chosen, preferred_element_type=F32)
        for part in range(2):
            scaled = product[:, part * width : (part + 1) * width] * (1.0 / windows)
            tiles[chunk * CHUNK + index, part] = scaled.astype(BF16)
            store(chunk * CHUNK + index, part).start()

    @pl.when(chunk == chunks - 1)
    def _():
        for bin_index in range(tiles.shape[0]):
            for part in range(2):
                store(bin_index, part).wait()


def multiply(count, places, held, swapped, windows):
    height = held[0].shape[1]
    depth, width = count * count * WINDOW_GROUP, height // 2
    vmem = pl.BlockSpec(memory_space=pltpu.VMEM)
    return pl.pallas_call(
        functools.partial(product_body, count, windows, places),
        out_shape=jax.ShapeDtypeStruct((F, 2, height, width), BF16),
        grid=(CHUNKS,),
        in_specs=[vmem] * (2 * len(held)),
        out_specs=pl.BlockSpec(memory_space=pl.ANY),
        scratch_shapes=[
            pltpu.VMEM((height, depth), BF16),
            pltpu.VMEM((depth, 2 * width), F32),
            pltpu.VMEM((F, 2, height, width), BF16),
            pltpu.SemaphoreType.DMA((F, 2)),
        ],
        compiler_params=pltpu.CompilerParams(vmem_limit_bytes=40 * 2**20),
        cost_estimate=pl.CostEstimate(
            flops=F * 4 * height * width * depth,
            bytes_accessed=F * 2 * height * width * 2,
            transcendentals=0,
        ),
        name="products",
    )(*held, *swapped)


def on_device(record, fir_taps, bins, offsets):
    row_count, col_count = lax.axis_size("row"), lax.axis_size("col")
    lines = col_count // 2
    windows = row_count * col_count

    def send(value, row_flip, line_flip, core_flip):
        pairs = []
        for row in range(row_count):
            for col in range(col_count):
                core, line = col % 2, col // 2
                target = 2 * (line ^ line_flip[core]) + (core ^ core_flip)
                pairs.append((row * col_count + col, (row ^ row_flip[core]) * col_count + target))
        return lax.ppermute(value, AXES, pairs)

    def swap(value):
        return send(value, (0, 0), (0, 0), 1)

    own = make_spectra(record, fir_taps, bins, offsets, row_count)
    to_send = pair_windows(hold(own, []), swap(own))
    turns = [0, *reversed(range(1, row_count))]
    pieces = {0: to_send[0]}
    for step in turns[1:]:
        pieces[step] = send(to_send[step], (step, 0), (0, step), 0)

    bits = [row_count >> shift for shift in range(1, row_count.bit_length())]
    packs, places, early = [], {}, []
    for step, piece in pieces.items():
        if step == turns[-1]:
            piece = hold(piece, early[1:2])
        held = {0: piece}
        for bit in bits:
            for slot in list(held):
                held[slot ^ bit] = send(held[slot], (0, bit), (bit, 0), 0)
        early.append(held[1])
        for order, slot in enumerate(held):
            places[step, slot] = (len(packs), order * 2 * ROWS)
        packs.append(pack(list(held.values())))
    return multiply(row_count, places, packs, [swap(value) for value in packs], windows)


def solution(mesh):
    placed = (P(("row", "col"), None), P(), P(), P(("row", "col")))
    return jax.shard_map(
        on_device,
        mesh=mesh,
        in_specs=placed,
        out_specs=P(None, None, "row", "col"),
        check_vma=False,
    )
```
